256 devices in a mesh: row: 32 (over z, x), col: 8 (over y, core).
Axes of the slice: x: 4, y: 4, z: 8, core: 2. Of those that a mesh axis runs over, the one named last changes fastest.
Arguments:
- rhs: float32 [8, 32, 256, 128], P(None, 'row'), may hold values from -6 to 6
- inverse_low: bfloat16 [7, 32, 256, 2, 8, 256], P(None, 'row', None, None, 'col'), as said below
- inverse_top: bfloat16 [1, 32, 256, 4, 8, 256], P(None, 'row', None, None, 'col'), as said below
- lower_one: bfloat16 [2, 32, 256, 4, 8, 256], P(None, 'row', None, None, 'col')
- lower_two: bfloat16 [1, 32, 256, 12, 8, 256], P(None, 'row', None, None, 'col')
- lower_top: bfloat16 [1, 32, 256, 28, 8, 256], P(None, 'row', None, None, 'col'), as said below
- block_rows: int32 [256, 64], replicated, may hold values from -1 to 255, as said below
Outputs:
- solution: float32 [8, 32, 256, 128], P(None, 'row')
The draws below stay inside these ranges and needn't reach their ends.
Inputs may be any that keep to these rules, and one draw needn't show every extreme that they name: `block_rows`: row j lists, in increasing order, distinct block rows of the separators that are ancestors of sep(j), then -1 to the end; the last block row 255 is listed by every block column below level 3. `inverse_low`: holds the full inverses of the separators' diagonal blocks. `inverse_top`: holds the full inverse of the top separator's diagonal block. `lower_top`: stored blocks that block_rows does not list hold values that are not entries of the factor.
All inputs are finite; a program needn't handle non-finite values.
Results may differ from the reference program's by a relative error of at most 0.0041.
Values may be sent and summed in bfloat16 or wider, within the bound.
No kernel may reach another device: no remote copies, remote signals or barrier semaphores. Data moves between devices by JAX's collectives and lax.ppermute only.
A program may use at most 64 MiB of HBM per device.

```python
import jax
import jax.numpy as jnp
import numpy as np
from jax import lax

BLOCK = 256
RHS = 128
SEP_BLOCKS = 16
NB = 256
MAXR = 64
N_ROW = 32
N_COL = 8


def separator_of(block_ids):
    return jnp.minimum(block_ids // SEP_BLOCKS, 14)


def parent_of(sep_ids):
    return jnp.where(sep_ids < 8, 8 + sep_ids // 2, jnp.where(sep_ids < 12, 12 + (sep_ids - 8) // 2, 14))


def cyclic(matrix):
    return matrix.reshape(matrix.shape[0] // N_ROW, N_ROW, BLOCK, matrix.shape[2] // N_COL, N_COL, BLOCK)


def inverse_blocks(noise, diagonal_vals, is_diag, sep_width):
    inner = jnp.arange(BLOCK, dtype=jnp.int32)
    same = inner[:, None] == inner[None, :]
    mask = is_diag[:, None, :, None] & same[None, :, None, :]
    return jnp.where(mask, diagonal_vals[:, :, None, None], 0.6 * noise / jnp.sqrt(1.0 * sep_width * BLOCK))


def draw_block_rows(key, part):
    key = jax.random.fold_in(key, 11)
    blocks = jnp.arange(NB, dtype=jnp.int32)
    col_sep = separator_of(blocks)[:, None]
    row_sep = separator_of(blocks)[None, :]
    first_up = parent_of(col_sep)
    second_up = parent_of(first_up)
    third_up = parent_of(second_up)
    ancestor = (row_sep != col_sep) & ((row_sep == first_up) | (row_sep == second_up) | (row_sep == third_up))
    coin = jax.random.randint(key, (NB, NB), 0, 2)
    chosen = ancestor & ((coin == 1) | (blocks[None, :] == NB - 1))
    score = jnp.where(chosen, blocks[None, :], NB + blocks[None, :])
    picked = jnp.sort(score, axis=1)[:, :MAXR]
    return jnp.where(picked < NB, picked, -1).astype(jnp.int32)


def draw_inverse_low(key, part):
    key = jax.random.fold_in(key, 21)
    first_key, second_key = jax.random.split(key)
    shape = (14 * SEP_BLOCKS, BLOCK, SEP_BLOCKS, BLOCK)
    noise = jax.random.normal(first_key, shape, jnp.float32)
    diagonal_vals = jax.random.uniform(second_key, (shape[0], BLOCK), jnp.float32, 0.5, 1.5)
    rows = jnp.arange(shape[0], dtype=jnp.int32)
    cols = jnp.arange(shape[2], dtype=jnp.int32)
    is_diag = (rows % SEP_BLOCKS)[:, None] == cols[None, :]
    return cyclic(inverse_blocks(noise, diagonal_vals, is_diag, SEP_BLOCKS)).astype(jnp.bfloat16)


def draw_inverse_top(key, part):
    key = jax.random.fold_in(key, 23)
    first_key, second_key = jax.random.split(key)
    shape = (2 * SEP_BLOCKS, BLOCK, 2 * SEP_BLOCKS, BLOCK)
    noise = jax.random.normal(first_key, shape, jnp.float32)
    diagonal_vals = jax.random.uniform(second_key, (shape[0], BLOCK), jnp.float32, 0.5, 1.5)
    rows = jnp.arange(shape[0], dtype=jnp.int32)
    is_diag = rows[:, None] == rows[None, :]
    return cyclic(inverse_blocks(noise, diagonal_vals, is_diag, 2 * SEP_BLOCKS)).astype(jnp.bfloat16)


def draw_lower_one(key, part):
    key = jax.random.fold_in(key, 31)
    shape = (4 * SEP_BLOCKS, BLOCK, 2 * SEP_BLOCKS, BLOCK)
    noise = jax.random.normal(key, shape, jnp.float32)
    return cyclic(0.7 * noise / jnp.sqrt(1.0 * SEP_BLOCKS * BLOCK)).astype(jnp.bfloat16)


def draw_lower_two(key, part):
    key = jax.random.fold_in(key, 33)
    shape = (2 * SEP_BLOCKS, BLOCK, 6 * SEP_BLOCKS, BLOCK)
    noise = jax.random.normal(key, shape, jnp.float32)
    return cyclic(0.7 * noise / jnp.sqrt(3.0 * SEP_BLOCKS * BLOCK)).astype(jnp.bfloat16)


def draw_lower_top(key, part):
    key = jax.random.fold_in(key, 35)
    shape = (2 * SEP_BLOCKS, BLOCK, 14 * SEP_BLOCKS, BLOCK)
    noise = jax.random.normal(key, shape, jnp.float32)
    return cyclic(0.7 * noise / jnp.sqrt(7.0 * SEP_BLOCKS * BLOCK)).astype(jnp.bfloat16)


def levels(stream_key, shape, shards, smallest, high):
    level = 1.0
    for dim, blocks in shards:
        steps = jax.random.uniform(jax.random.fold_in(jax.random.fold_in(stream_key, 6), dim), (blocks,), jnp.float32, smallest / len(shards), high / len(shards))
        level = level * jnp.repeat(jnp.exp(steps), shape[dim] // blocks).reshape((-1,) + (1,) * (len(shape) - 1 - dim))
    return level


def scatter_about(own_key, extent, deviation, most, cuts=(), kind=jnp.bfloat16):
    array = jax.random.normal(own_key, extent, jnp.float32) * deviation
    if len(cuts) > 0:
        array = levels(own_key, extent, cuts, -0.22, 0.18) * array
    return jnp.clip(array, min=-most, max=most).astype(kind)


def setup_inputs(seed: int = 0) -> dict:
    key_of = jax.random.split(jax.random.key(seed), 8)
    return {
        "rhs": scatter_about(key_of[0], (NB // N_ROW, N_ROW, BLOCK, RHS), 1.0, 6.0, ((1, 32),), jnp.float32),
        "inverse_low": draw_inverse_low(jax.random.fold_in(key_of[7], 71), 0),
        "inverse_top": draw_inverse_top(jax.random.fold_in(key_of[7], 71), 0),
        "lower_one": draw_lower_one(jax.random.fold_in(key_of[7], 71), 0),
        "lower_two": draw_lower_two(jax.random.fold_in(key_of[7], 71), 0),
        "lower_top": draw_lower_top(jax.random.fold_in(key_of[7], 71), 0),
        "block_rows": draw_block_rows(jax.random.fold_in(key_of[7], 71), 0),
    }


def masked_rows(tile, keep, columns):
    flat = columns.reshape(-1, columns.shape[-1])

    def one_row(pair):
        row_tile, row_keep = pair
        masked = row_tile * row_keep.astype(row_tile.dtype)[None, :, None]
        return jnp.dot(masked.reshape(row_tile.shape[0], -1), flat, preferred_element_type=jnp.float32)

    return lax.map(one_row, (tile, keep))


def reference(rhs, inverse_low, inverse_top, lower_one, lower_two, lower_top, block_rows):
    sep_count = SEP_BLOCKS
    vector = rhs.reshape(NB, BLOCK, RHS)
    diag_low = inverse_low.reshape(14 * sep_count, BLOCK, sep_count, BLOCK)
    diag_top = inverse_top.reshape(2 * sep_count * BLOCK, 2 * sep_count * BLOCK)
    band_one = lower_one.reshape(4 * sep_count, BLOCK, 2 * sep_count, BLOCK)
    band_two = lower_two.reshape(2 * sep_count, BLOCK, 6 * sep_count, BLOCK)
    band_top = lower_top.reshape(2 * sep_count, BLOCK, 14 * sep_count, BLOCK)
    blocks = jnp.arange(NB, dtype=jnp.int32)
    listed = jnp.any(block_rows[:, :, None] == blocks[None, None, :], axis=1)
    starts = [0, 8 * sep_count, 12 * sep_count, 14 * sep_count, 16 * sep_count]
    sent = jnp.zeros((NB, BLOCK, RHS), jnp.bfloat16)
    pieces = []
    for level in range(4):
        low, high = starts[level], starts[level + 1]
        if level == 0:
            reduced = vector[low:high].astype(jnp.bfloat16)
        else:
            sums = []
            if level == 1:
                for separator in range(8, 12):
                    rows = np.arange(separator * sep_count, (separator + 1) * sep_count).astype(np.int32)
                    first = 2 * (separator - 8) * sep_count
                    cols = np.arange(first, first + 2 * sep_count).astype(np.int32)
                    keep = listed[cols][:, rows].T
                    tile = band_one[(separator - 8) * sep_count:(separator - 7) * sep_count]
                    sums.append(masked_rows(tile, keep, sent[cols]))
            elif level == 2:
                for separator in range(12, 14):
                    rows = np.arange(separator * sep_count, (separator + 1) * sep_count).astype(np.int32)
                    grand = 4 * (separator - 12) * sep_count
                    child = (8 + 2 * (separator - 12)) * sep_count
                    cols = np.concatenate([np.arange(grand, grand + 4 * sep_count), np.arange(child, child + 2 * sep_count)]).astype(np.int32)
                    keep = listed[cols][:, rows].T
                    tile = band_two[(separator - 12) * sep_count:(separator - 11) * sep_count]
                    sums.append(masked_rows(tile, keep, sent[cols]))
            else:
                rows = np.arange(low, high).astype(np.int32)
                cols = np.arange(0, 14 * sep_count).astype(np.int32)
                keep = listed[cols][:, rows].T
                sums.append(masked_rows(band_top, keep, sent[cols]))
            lower_sum = jnp.concatenate(sums, axis=0)
            reduced = (vector[low:high] - lower_sum).astype(jnp.bfloat16)
        if level < 3:
            solved = []
            for separator in range(low // sep_count, high // sep_count):
                inverse = diag_low[separator * sep_count:(separator + 1) * sep_count].reshape(sep_count * BLOCK, sep_count * BLOCK)
                offset = separator * sep_count - low
                part_u = reduced[offset:offset + sep_count].reshape(sep_count * BLOCK, RHS)
                solved.append(jnp.dot(inverse, part_u, preferred_element_type=jnp.float32).reshape(sep_count, BLOCK, RHS))
            solved = jnp.concatenate(solved, axis=0)
        else:
            solved = jnp.dot(diag_top, reduced.reshape(-1, RHS), preferred_element_type=jnp.float32).reshape(2 * sep_count, BLOCK, RHS)
        pieces.append(solved)
        sent = sent.at[low:high].set(solved.astype(jnp.bfloat16))
    return jnp.concatenate(pieces, axis=0).reshape(NB // N_ROW, N_ROW, BLOCK, RHS)
```

```python
import jax
import jax.numpy as jnp
from jax import lax
from jax.experimental import pallas as pl
from jax.experimental.pallas import tpu as pltpu
from jax.sharding import PartitionSpec as P

AXES = ("row", "col")
BF = jnp.bfloat16
F32 = jnp.float32
N = 256


def ring(a, b, n):
    d = (a - b) % n
    return min(d, n - d)


def row_hops(a, b):
    return ring(a // 4, b // 4, 8) + ring(a % 4, b % 4, 4)


def col_hops(a, b):
    return 2 * ring(a // 2, b // 2, 4) + (a % 2 != b % 2)


def spread_pairs(shift):
    pairs = []
    for m in range(4):
        for q in range(8):
            source = 8 * (m ^ shift) + q
            rows = sorted(range(8 * m, 8 * m + 8), key=lambda o: -row_hops(o, source))
            cols = sorted(range(8), key=lambda t: col_hops(t, q))
            pairs += [(source * 8 + t, o * 8 + q) for o, t in zip(rows, cols)]
    return sorted(pairs)


def turn_table():
    table = []
    for r in range(8):
        rows = sorted(range(8), key=lambda o: -row_hops(o, r))
        cols = sorted(range(8), key=lambda t: col_hops(t, r))
        line = [0] * 8
        for o, t in zip(rows, cols):
            line[t] = o
        table.append(line)
    return table


def turn_pairs():
    table = turn_table()
    return [
        ((8 * m + r) * 8 + t, (8 * m + table[r][t]) * 8 + r)
        for m in range(4)
        for r in range(8)
        for t in range(8)
    ]


def send(value, pairs):
    return lax.ppermute(value, AXES, pairs)


def dot(tile, block):
    return lax.dot_general(tile, block, (((1,), (1,)), ((), ())), preferred_element_type=F32)


def at(array, index, axis=0):
    return lax.dynamic_index_in_dim(array, index, axis, keepdims=False)


def params():
    return pltpu.CompilerParams(vmem_limit_bytes=24 * 1024 * 1024)


def whole(*_):
    return pl.BlockSpec(memory_space=pltpu.VMEM)


def diagonal0(place, near, far, tiles):
    def kernel(s, near_ref, far_ref, tile_ref, out_ref):
        e = s[1]
        for a in range(4):
            value = dot(tile_ref[a, e], near_ref[a]) + dot(tile_ref[a, 1 - e], far_ref[a])
            out_ref[:, a] = value.T.reshape(8, 16, 256).astype(BF)

    return pl.pallas_call(
        kernel,
        out_shape=jax.ShapeDtypeStruct((8, 4, 16, 256), BF),
        in_specs=[pl.BlockSpec(memory_space=pltpu.SMEM), whole(), whole(), whole()],
        out_specs=whole(),
        compiler_params=params(),
        name="diagonal0",
    )(place, near, far, tiles)


def lower0(place, keep, slices, one, two, last):
    def kernel(s, k, x_ref, one_ref, two_ref, last_ref, out_ref, acc):
        c, h = pl.program_id(0), s[3]

        def term(pairs):
            tiles = jnp.concatenate([tile for _, tile, _ in pairs], axis=1)
            blocks = []
            for a0, _, flag in pairs:
                block = jnp.concatenate([x_ref[p, a0] for p in range(8)], axis=0)
                blocks.append(jnp.where(flag != 0, block, jnp.zeros_like(block)))
            return dot(tiles, jnp.concatenate(blocks, axis=1))

        sums = [
            term([(h, one_ref[0, 0], k[4 * h + c])]),
            term([(2 + h, one_ref[1, 0], k[32 + 8 + 4 * h + c])]),
            term([(2 * h + b, two_ref[b, 0], k[64 + 8 * h + 4 * b + c]) for b in range(2)]),
            term([(a0, last_ref[a0, 0], k[96 + 4 * a0 + c]) for a0 in range(4)]),
        ]

        @pl.when(c == 0)
        def _():
            for i in range(4):
                acc[i] = sums[i]

        @pl.when(c != 0)
        def _():
            for i in range(4):
                acc[i] += sums[i]

        @pl.when(c == 3)
        def _():
            for i in range(4):
                value = acc[i].T.astype(BF)
                for p in range(8):
                    out_ref[s[4 + p], i] = value[16 * p : 16 * p + 16]

    return pl.pallas_call(
        kernel,
        out_shape=jax.ShapeDtypeStruct((8, 4, 16, 256), BF),
        grid_spec=pltpu.PrefetchScalarGridSpec(
            num_scalar_prefetch=2,
            grid=(4,),
            in_specs=[
                pl.BlockSpec((8, 4, 16, 256), lambda c, s, k: (c, 0, 0, 0)),
                pl.BlockSpec((2, 1, 256, 256), lambda c, s, k: (0, c, 0, 0)),
                pl.BlockSpec((2, 1, 256, 256), lambda c, s, k: (0, c, 0, 0)),
                pl.BlockSpec((4, 1, 256, 256), lambda c, s, k: (0, c, 0, 0)),
            ],
            out_specs=pl.BlockSpec((8, 4, 16, 256), lambda c, s, k: (0, 0, 0, 0)),
            scratch_shapes=[pltpu.VMEM((4, 256, 128), F32)],
        ),
        compiler_params=params(),
        name="lower0",
    )(place, keep, slices, one, two, last)


def multiply(place, terms, base, n_out, copies, dtype, name, token=None):
    steps = terms[0][3]

    def kernel(s, *refs):
        step = pl.program_id(0)
        copy_ref, out_ref, acc = refs[-3:]
        h = s[3]
        tiles, blocks = [[] for _ in range(n_out)], [[] for _ in range(n_out)]
        for n, (_, _, _, _, _, picks) in enumerate(terms):
            x_ref, tile_ref = refs[2 * n : 2 * n + 2]
            for t, c, a, o in picks(step, h):
                for j in range(8):
                    tiles[o].append(tile_ref[j, t])
                    blocks[o].append(x_ref[8 * c + j, a])
        for o in range(n_out):
            value = dot(jnp.concatenate(tiles[o], axis=1), jnp.concatenate(blocks[o], axis=1))

            @pl.when(step == 0)
            def _():
                acc[o] = value

            @pl.when(step != 0)
            def _():
                acc[o] += value

        @pl.when(step == steps - 1)
        def _():
            for o in range(n_out):
                value = acc[o].T
                if base is not None:
                    value = refs[2 * len(terms)][o] - value
                out_ref[o] = value
                cast = value.astype(dtype)
                for r in range(copies):
                    copy_ref[r, o] = cast

    args, specs, size = [], [], 0
    for x, tiles, first, _, count, _ in terms:
        args += [x, tiles]
        specs.append(pl.BlockSpec(x.shape, lambda i, s: (0, 0, 0, 0)))
        specs.append(
            pl.BlockSpec((8, count, 256, 256), lambda i, s, f=first // count: (0, f + i, 0, 0))
        )
        size += 8 * count * steps * 256 * 256
    if base is not None:
        args.append(base)
        specs.append(pl.BlockSpec(base.shape, lambda i, s: (0, 0, 0)))
    if token is not None:
        args.append(token)
        specs.append(pl.BlockSpec(token.shape, lambda i, s: (0, 0)))
    return pl.pallas_call(
        kernel,
        out_shape=(
            jax.ShapeDtypeStruct((copies, n_out, 16, 256), dtype),
            jax.ShapeDtypeStruct((n_out, 16, 256), F32),
        ),
        grid_spec=pltpu.PrefetchScalarGridSpec(
            num_scalar_prefetch=1,
            grid=(steps,),
            in_specs=specs,
            out_specs=(
                pl.BlockSpec((copies, n_out, 16, 256), lambda i, s: (0, 0, 0, 0)),
                pl.BlockSpec((n_out, 16, 256), lambda i, s: (0, 0, 0)),
            ),
            scratch_shapes=[pltpu.VMEM((n_out, 256, 16), F32)],
        ),
        compiler_params=params(),
        cost_estimate=pl.CostEstimate(flops=256 * size, bytes_accessed=2 * size, transcendentals=0),
        name=name,
    )(place, *args)


def assemble_early(slices):
    def kernel(x_ref, out_ref):
        out_ref[0] = x_ref[:, 0].reshape(128, 256).T

    return pl.pallas_call(
        kernel,
        out_shape=jax.ShapeDtypeStruct((8, 256, 128), F32),
        grid=(6,),
        in_specs=[pl.BlockSpec((8, 1, 16, 256), lambda i: (0, i, 0, 0))],
        out_specs=pl.BlockSpec((1, 256, 128), lambda i: (i, 0, 0)),
        compiler_params=params(),
        name="assemble_early",
    )(slices)


def assemble_late(early, slices):
    def kernel(x_ref, _, out_ref):
        out_ref[0] = x_ref[:, 0].reshape(128, 256).T

    return pl.pallas_call(
        kernel,
        out_shape=jax.ShapeDtypeStruct((8, 256, 128), F32),
        grid=(2,),
        in_specs=[
            pl.BlockSpec((8, 1, 16, 256), lambda i: (0, i, 0, 0)),
            pl.BlockSpec(memory_space=pl.ANY),
        ],
        out_specs=pl.BlockSpec((1, 256, 128), lambda i: (6 + i, 0, 0)),
        input_output_aliases={1: 0},
        compiler_params=params(),
        name="assemble_late",
    )(slices, early)


HALVES = [list(range(16)), list(range(16, 32))]


def exchange(copies, axis, groups=None):
    return lax.all_to_all(copies, axis, 0, 0, tiled=True, axis_index_groups=groups)


def swap(value, mask):
    return send(value, [(i, i ^ mask) for i in range(256)])


def finish0(sums, upper, token):
    def kernel(x_ref, upper_ref, _, copy_ref, two_ref, three_ref):
        value = upper_ref[...] - jnp.sum(x_ref[...].astype(F32), axis=0)
        two_ref[...] = value[2:3]
        three_ref[...] = value[3:4]
        cast = value[0:2].astype(BF)
        for r in range(16):
            copy_ref[r] = cast

    slot = jax.ShapeDtypeStruct((1, 16, 256), F32)
    return pl.pallas_call(
        kernel,
        out_shape=(jax.ShapeDtypeStruct((16, 2, 16, 256), BF), slot, slot),
        compiler_params=params(),
        name="finish0",
    )(sums, upper, token)


def arrived(tiles):
    return tiles[0, 0, 0:16, 0:128]


def body(rhs, inverse_low, inverse_top, lower_one, lower_two, lower_top, block_rows):
    row = lax.axis_index("row")
    col = lax.axis_index("col")
    m, h, e, core = row // 8, row // 16, row // 8 % 2, col % 2
    table = turn_table()
    owner = [[line.index(p) for p in range(8)] for line in table]
    place = jnp.concatenate(
        [jnp.stack([m, e, core, h]), at(jnp.array(owner, jnp.int32), col), col[None]]
    ).astype(jnp.int32)
    sent0 = jnp.swapaxes(rhs[0:4, 0], 1, 2).astype(BF)
    near = send(sent0, spread_pairs(0))
    far = send(sent0, spread_pairs(1))

    lists = at(block_rows.reshape(32, 8, 64), col, 1)
    targets = jnp.stack([128 + row, 160 + row, 192 + row, 224 + row])
    listed = jnp.any(lists[None] == targets[:, None, None], axis=-1)
    keep = listed.astype(jnp.int32).reshape(128)

    def masked(tiles, flags):
        return jnp.where(flags[:, None, None], tiles, jnp.zeros_like(tiles))

    two = jnp.swapaxes(lower_two[0, 0, :, :, 0, :], 0, 1).reshape(3, 4, 256, 256)
    last = jnp.swapaxes(lower_top[0, 0, :, :, 0, :], 0, 1).reshape(7, 4, 256, 256)
    first = jnp.concatenate(
        [
            jnp.swapaxes(inverse_low[4:6, 0, :, :, 0, :], 1, 2).reshape(4, 256, 256),
            masked(two[2], lax.dynamic_slice(listed[2], (16 + 4 * h,), (4,))),
            jnp.swapaxes(inverse_low[6, 0, :, :, 0, :], 0, 1),
        ]
    )
    gate = near[0, 0, 0] * 0
    first = lax.all_gather(first + gate, "col")
    low, one, upper = lax.optimization_barrier((inverse_low[0:4], lower_one, rhs[4:8, 0]))
    low = jnp.swapaxes(low[:, 0, :, :, 0, :], 1, 2)
    one = jnp.swapaxes(one[:, 0, :, :, 0, :], 1, 2)
    upper = lax.dynamic_slice(jnp.swapaxes(upper, 1, 2), (0, 16 * col, 0), (4, 16, 256))
    near, far, last_later, inverse_top = lax.optimization_barrier((near, far, last[4:7], inverse_top))
    second = lax.all_gather(masked(last_later.reshape(12, 256, 256), listed[3, 16:28]) + gate, "col")
    third = lax.all_gather(jnp.swapaxes(inverse_top[0, 0, :, :, 0, :], 0, 1) + gate, "col")

    near, far, keep, upper, one = lax.optimization_barrier((near, far, keep, upper, one))

    sums = exchange(diagonal0(place, near, far, low), "col")
    solved0 = jnp.sum(sums.astype(F32), axis=0)
    slices = send(solved0.astype(BF), turn_pairs())
    slices, one = lax.optimization_barrier((slices, one))
    slices = exchange(jnp.broadcast_to(slices, (32, 4, 16, 256)), "row")
    sums = exchange(lower0(place, keep, slices, one, two, last), "col")
    copies, base2, base3 = finish0(sums, upper, arrived(first))

    reduced = exchange(copies, "row", HALVES)
    copies, solved1 = multiply(
        place, [(reduced, first, 0, 1, 4, lambda i, h: [(t, t % 2, t // 2, t // 2) for t in range(4)])], None, 2, 32, BF, "diagonal1"
    )
    x1 = exchange(copies, "row")
    early = lax.all_gather(jnp.concatenate([solved0, solved1, solved1]), "col")

    copies, _ = multiply(
        place, [(x1, first, 4, 4, 1, lambda i, h: [(0, i, h, 0)])], base2, 1, 16, BF, "lower2"
    )
    reduced = exchange(copies, "row", HALVES)
    copies, solved2 = multiply(
        place, [(reduced, first, 8, 2, 1, lambda i, h: [(0, i, 0, 0)])], None, 1, 32, BF, "diagonal2", arrived(second)
    )
    x2 = exchange(copies, "row")

    copies, _ = multiply(
        place,
        [
            (x1, second, 0, 4, 2, lambda i, h: [(t, (2 * i + t) % 4, i // 2, 0) for t in range(2)]),
            (x2, second, 8, 4, 1, lambda i, h: [(0, i, 0, 0)]),
        ],
        base3, 1, 32, BF, "lower3", arrived(third),
    )
    reduced = exchange(copies, "row")
    _, solved3 = multiply(
        place, [(reduced, third, 0, 4, 1, lambda i, h: [(0, i, 0, 0)])], None, 1, 1, BF, "diagonal3"
    )
    late = jnp.concatenate([solved2, solved3])
    late = exchange(jnp.broadcast_to(late, (8, 2, 16, 256)), "col")
    return assemble_late(assemble_early(early), late)[:, None]


def solution(mesh):
    return jax.shard_map(
        body,
        mesh=mesh,
        in_specs=(
            P(None, "row", None, None),
            P(None, "row", None, None, "col", None),
            P(None, "row", None, None, "col", None),
            P(None, "row", None, None, "col", None),
            P(None, "row", None, None, "col", None),
            P(None, "row", None, None, "col", None),
            P(),
        ),
        out_specs=P(None, "row", None, None),
        check_vma=False,
    )
```

```python
import jax
import jax.numpy as jnp
from jax import lax
from jax.experimental import pallas as pl
from jax.experimental.pallas import tpu as pltpu
from jax.sharding import PartitionSpec as P

AXES = ("row", "col")
BF = jnp.bfloat16
F32 = jnp.float32
N = 256


def ring(a, b, n):
    d = (a - b) % n
    return min(d, n - d)


def row_hops(a, b):
    return ring(a // 4, b // 4, 8) + ring(a % 4, b % 4, 4)


def col_hops(a, b):
    return 2 * ring(a // 2, b // 2, 4) + (a % 2 != b % 2)


def spread_pairs(shift):
    pairs = []
    for m in range(4):
        for q in range(8):
            source = 8 * (m ^ shift) + q
            rows = sorted(range(8 * m, 8 * m + 8), key=lambda o: -row_hops(o, source))
            cols = sorted(range(8), key=lambda t: col_hops(t, q))
            pairs += [(source * 8 + t, o * 8 + q) for o, t in zip(rows, cols)]
    return sorted(pairs)


def turn_table():
    table = []
    for r in range(8):
        rows = sorted(range(8), key=lambda o: -row_hops(o, r))
        cols = sorted(range(8), key=lambda t: col_hops(t, r))
        line = [0] * 8
        for o, t in zip(rows, cols):
            line[t] = o
        table.append(line)
    return table


def turn_pairs():
    table = turn_table()
    return [
        ((8 * m + r) * 8 + t, (8 * m + table[r][t]) * 8 + r)
        for m in range(4)
        for r in range(8)
        for t in range(8)
    ]


def send(value, pairs):
    return lax.ppermute(value, AXES, pairs)


def dot(tile, block):
    return lax.dot_general(tile, block, (((1,), (1,)), ((), ())), preferred_element_type=F32)


def at(array, index, axis=0):
    return lax.dynamic_index_in_dim(array, index, axis, keepdims=False)


def params(mib=24):
    return pltpu.CompilerParams(vmem_limit_bytes=mib * 1024 * 1024)


def whole(*_):
    return pl.BlockSpec(memory_space=pltpu.VMEM)


def diagonal0(place, near, far, tiles, ready, passed):
    count = len(ready)

    def kernel(s, near_ref, far_ref, tile_ref, *refs):
        e, out_ref = s[1], refs[count + len(passed)]
        for a in range(4):
            value = jnp.dot(tile_ref[a, e], near_ref[a], preferred_element_type=F32)
            value += jnp.dot(tile_ref[a, 1 - e], far_ref[a], preferred_element_type=F32)
            out_ref[:, a] = value.T.reshape(8, 16, 256).astype(BF)

    anywhere = pl.BlockSpec(memory_space=pl.ANY)
    return pl.pallas_call(
        kernel,
        out_shape=(jax.ShapeDtypeStruct((8, 4, 16, 256), BF),)
        + tuple(jax.ShapeDtypeStruct(value.shape, value.dtype) for value in passed),
        in_specs=[pl.BlockSpec(memory_space=pltpu.SMEM), whole(), whole(), whole()]
        + [anywhere] * (count + len(passed)),
        out_specs=(whole(),) + (anywhere,) * len(passed),
        input_output_aliases={4 + count + i: 1 + i for i in range(len(passed))},
        compiler_params=params(),
        name="diagonal0",
    )(place, near, far, tiles, *ready, *passed)


def lower0(place, keep, slices, one, two, last):
    def kernel(s, k, x_ref, one_ref, two_ref, last_ref, out_ref, acc):
        c, h = pl.program_id(0), s[3]

        def term(pairs):
            tiles = jnp.concatenate([tile for _, tile, _ in pairs], axis=1)
            blocks = []
            for a0, _, flag in pairs:
                block = jnp.concatenate([x_ref[p % 4, p // 4, a0] for p in range(8)], axis=0)
                blocks.append(jnp.where(flag != 0, block, jnp.zeros_like(block)))
            return dot(tiles, jnp.concatenate(blocks, axis=1))

        sums = [
            term([(h, one_ref[0, 0], k[4 * h + c])]),
            term([(2 + h, one_ref[1, 0], k[32 + 8 + 4 * h + c])]),
            term([(2 * h + b, two_ref[b, 0], k[64 + 8 * h + 4 * b + c]) for b in range(2)]),
            term([(a0, last_ref[a0, 0], k[96 + 4 * a0 + c]) for a0 in range(4)]),
        ]

        @pl.when(c == 0)
        def _():
            for i in range(4):
                acc[i] = sums[i]

        @pl.when(c != 0)
        def _():
            for i in range(4):
                acc[i] += sums[i]

        @pl.when(c == 3)
        def _():
            for i in range(4):
                value = acc[i].T.astype(BF)
                for p in range(8):
                    out_ref[s[4 + p], i] = value[16 * p : 16 * p + 16]

    return pl.pallas_call(
        kernel,
        out_shape=jax.ShapeDtypeStruct((8, 4, 16, 256), BF),
        grid_spec=pltpu.PrefetchScalarGridSpec(
            num_scalar_prefetch=2,
            grid=(4,),
            in_specs=[
                pl.BlockSpec((4, 2, 4, 16, 256), lambda c, s, k: (0, c, 0, 0, 0)),
                pl.BlockSpec((2, 1, 256, 256), lambda c, s, k: (0, c, 0, 0)),
                pl.BlockSpec((2, 1, 256, 256), lambda c, s, k: (0, c, 0, 0)),
                pl.BlockSpec((4, 1, 256, 256), lambda c, s, k: (0, c, 0, 0)),
            ],
            out_specs=pl.BlockSpec((8, 4, 16, 256), lambda c, s, k: (0, 0, 0, 0)),
            scratch_shapes=[pltpu.VMEM((4, 256, 128), F32)],
        ),
        compiler_params=params(),
        name="lower0",
    )(place, keep, slices, one, two, last)


def multiply(place, terms, base, n_out, copies, name, dtype=BF, early=None):
    steps = terms[0][3]
    early = early or ()
    lead = sum(value.shape[0] for value in early)
    total = n_out if not early else 8

    def kernel(s, *refs):
        step = pl.program_id(0)
        copy_ref, out_ref, acc = refs[-3:]
        h = s[3]
        tiles, blocks = [[] for _ in range(n_out)], [[] for _ in range(n_out)]
        for n, (_, _, _, _, _, picks) in enumerate(terms):
            x_ref, tile_ref = refs[2 * n : 2 * n + 2]
            for t, c, a, o in picks(step, h):
                for j in range(8):
                    tiles[o].append(tile_ref[j, t])
                    blocks[o].append(x_ref[8 * c + j, a])
        for o in range(n_out):
            value = dot(jnp.concatenate(tiles[o], axis=1), jnp.concatenate(blocks[o], axis=1))

            @pl.when(step == 0)
            def _():
                acc[o] = value

            @pl.when(step != 0)
            def _():
                acc[o] += value

        @pl.when(step == steps - 1)
        def _():
            for o in range(n_out):
                value = acc[o].T
                if base is not None:
                    value = refs[2 * len(terms)][o] - value
                out_ref[lead + o] = value
                cast = value.astype(dtype)
                for r in range(copies):
                    copy_ref[r, o] = cast
            if early:
                out_ref[0:4] = refs[2 * len(terms)][...]
                out_ref[4:6] = refs[2 * len(terms) + 1][...]
                out_ref[7:8] = jnp.zeros((1, 16, 256), F32)

    args, specs, size = [], [], 0
    for x, tiles, first, _, count, _ in terms:
        args += [x, tiles]
        specs.append(pl.BlockSpec(x.shape, lambda i, s: (0, 0, 0, 0)))
        specs.append(
            pl.BlockSpec((8, count, 256, 256), lambda i, s, f=first // count: (0, f + i, 0, 0))
        )
        size += 8 * count * steps * 256 * 256
    if base is not None:
        args.append(base)
        specs.append(pl.BlockSpec(base.shape, lambda i, s: (0, 0, 0)))
    for value in early:
        args.append(value)
        specs.append(pl.BlockSpec(value.shape, lambda i, s: (0, 0, 0)))
    return pl.pallas_call(
        kernel,
        out_shape=(
            jax.ShapeDtypeStruct((copies, n_out, 16, 256), dtype),
            jax.ShapeDtypeStruct((total, 16, 256), F32),
        ),
        grid_spec=pltpu.PrefetchScalarGridSpec(
            num_scalar_prefetch=1,
            grid=(steps,),
            in_specs=specs,
            out_specs=(
                pl.BlockSpec((copies, n_out, 16, 256), lambda i, s: (0, 0, 0, 0)),
                pl.BlockSpec((total, 16, 256), lambda i, s: (0, 0, 0)),
            ),
            scratch_shapes=[pltpu.VMEM((n_out, 256, 16), F32)],
        ),
        compiler_params=params(),
        cost_estimate=pl.CostEstimate(flops=256 * size, bytes_accessed=2 * size, transcendentals=0),
        name=name,
    )(place, *args)


def assemble_early(slices):
    def kernel(x_ref, out_ref):
        out_ref[0] = x_ref[:, 0].reshape(128, 256).T

    return pl.pallas_call(
        kernel,
        out_shape=jax.ShapeDtypeStruct((8, 256, 128), F32),
        grid=(7,),
        in_specs=[pl.BlockSpec((8, 1, 16, 256), lambda i: (0, i, 0, 0))],
        out_specs=pl.BlockSpec((1, 256, 128), lambda i: (i, 0, 0)),
        compiler_params=params(),
        name="assemble_early",
    )(slices)


def assemble_late(early, slices):
    def kernel(x_ref, _, out_ref):
        out_ref[0] = x_ref[:, 0].reshape(128, 256).T

    return pl.pallas_call(
        kernel,
        out_shape=jax.ShapeDtypeStruct((8, 256, 128), F32),
        grid=(1,),
        in_specs=[
            pl.BlockSpec((8, 1, 16, 256), lambda i: (0, i, 0, 0)),
            pl.BlockSpec(memory_space=pl.ANY),
        ],
        out_specs=pl.BlockSpec((1, 256, 128), lambda i: (7 + i, 0, 0)),
        input_output_aliases={1: 0},
        compiler_params=params(),
        name="assemble_late",
    )(slices, early)


HALVES = [list(range(16)), list(range(16, 32))]
ALONG_Z = [[4 * z + x for z in range(8)] for x in range(4)]
ALONG_X = [[4 * z + x for x in range(4)] for z in range(8)]


def exchange(copies, axis, groups=None):
    return lax.all_to_all(copies, axis, 0, 0, tiled=True, axis_index_groups=groups)


def swap(value, mask):
    return send(value, [(i, i ^ mask) for i in range(256)])


def finish0(sums, upper):
    def kernel(x_ref, upper_ref, copy_ref, two_ref, three_ref):
        value = upper_ref[...] - jnp.sum(x_ref[...].astype(F32), axis=0)
        two_ref[...] = value[2:3]
        three_ref[...] = value[3:4]
        cast = value[0:2].astype(BF)
        for r in range(16):
            copy_ref[r] = cast

    slot = jax.ShapeDtypeStruct((1, 16, 256), F32)
    return pl.pallas_call(
        kernel,
        out_shape=(jax.ShapeDtypeStruct((16, 2, 16, 256), BF), slot, slot),
        compiler_params=params(),
        name="finish0",
    )(sums, upper)


def body(rhs, inverse_low, inverse_top, lower_one, lower_two, lower_top, block_rows):
    row = lax.axis_index("row")
    col = lax.axis_index("col")
    m, h, e, core = row // 8, row // 16, row // 8 % 2, col % 2
    table = turn_table()
    owner = [[line.index(p) for p in range(8)] for line in table]
    place = jnp.concatenate(
        [jnp.stack([m, e, core, h]), at(jnp.array(owner, jnp.int32), col), col[None]]
    ).astype(jnp.int32)
    sent0 = rhs[0:4, 0].astype(BF)
    near = send(sent0, spread_pairs(0))
    far = send(sent0, spread_pairs(1))

    lists = at(block_rows.reshape(32, 8, 64), col, 1)

    def listed(block_row, first, count):
        return jnp.any(lax.dynamic_slice(lists, (first, 0), (count, 64)) == block_row, axis=-1)

    def masked(tiles, flags):
        return jnp.where(flags[:, None, None], tiles, jnp.zeros_like(tiles))

    low = lax.optimization_barrier(jnp.swapaxes(inverse_low[:, 0, :, :, 0, :], 1, 2))
    two = jnp.swapaxes(lower_two[0, 0, :, :, 0, :], 0, 1).reshape(3, 4, 256, 256)
    last = jnp.swapaxes(lower_top[0, 0, :, :, 0, :], 0, 1).reshape(7, 4, 256, 256)
    low1, low2 = low[4:6].reshape(4, 256, 256), low[6]
    two1 = masked(two[2], listed(192 + row, 16 + 4 * h, 4))
    first = lax.all_gather(jnp.concatenate([low1, two1, low2]), "col")
    one = jnp.swapaxes(lower_one[:, 0, :, :, 0, :], 1, 2)
    upper = lax.dynamic_slice(jnp.swapaxes(rhs[4:8, 0], 1, 2), (0, 16 * col, 0), (4, 16, 256))
    targets = jnp.stack([128 + row, 160 + row, 192 + row, 224 + row])
    keep = jnp.any(lists[None] == targets[:, None, None], axis=-1).astype(jnp.int32).reshape(128)

    second = masked(last[4:7].reshape(12, 256, 256), listed(224 + row, 16, 12))
    third = jnp.swapaxes(inverse_top[0, 0, :, :, 0, :], 0, 1)

    part, second, third = diagonal0(place, near, far, low[0:4], (one, upper, keep), (second, third))
    second, third = [lax.all_gather(value, "col") for value in (second, third)]
    sums = exchange(part, "col")
    solved0 = jnp.sum(sums.astype(F32), axis=0)
    slices = send(solved0.astype(BF), turn_pairs())
    slices = exchange(jnp.broadcast_to(slices, (8, 4, 16, 256)), "row", ALONG_Z)
    slices = exchange(jnp.broadcast_to(slices, (4, 8, 4, 16, 256)), "row", ALONG_X)
    sums = exchange(lower0(place, keep, slices, one, two, last), "col")
    copies, base2, base3 = finish0(sums, upper)

    reduced = exchange(copies, "row", HALVES)
    copies, solved1 = multiply(
        place, [(reduced, first, 0, 1, 4, lambda i, h: [(t, t % 2, t // 2, t // 2) for t in range(4)])], None, 2, 32, "diagonal1"
    )
    x1 = exchange(copies, "row")

    copies, _ = multiply(
        place, [(x1, first, 4, 4, 1, lambda i, h: [(0, i, h, 0)])], base2, 1, 16, "lower2"
    )
    reduced = exchange(copies, "row", HALVES)
    copies, solved2 = multiply(
        place, [(reduced, first, 8, 2, 1, lambda i, h: [(0, i, 0, 0)])], None, 1, 32, "diagonal2", early=(solved0, solved1)
    )
    x2 = exchange(copies, "row")
    early = lax.all_gather(solved2, "col")

    copies, _ = multiply(
        place,
        [
            (x1, second, 0, 4, 2, lambda i, h: [(t, (2 * i + t) % 4, i // 2, 0) for t in range(2)]),
            (x2, second, 8, 4, 1, lambda i, h: [(0, i, 0, 0)]),
        ],
        base3, 1, 32, "lower3",
    )
    reduced = exchange(copies, "row")
    copies, _ = multiply(
        place, [(reduced, third, 0, 4, 1, lambda i, h: [(0, i, 0, 0)])], None, 1, 8, "diagonal3", dtype=F32
    )
    late = exchange(copies, "col")
    return assemble_late(assemble_early(early), late)[:, None]


def solution(mesh):
    return jax.shard_map(
        body,
        mesh=mesh,
        in_specs=(
            P(None, "row", None, None),
            P(None, "row", None, None, "col", None),
            P(None, "row", None, None, "col", None),
            P(None, "row", None, None, "col", None),
            P(None, "row", None, None, "col", None),
            P(None, "row", None, None, "col", None),
            P(),
        ),
        out_specs=P(None, "row", None, None),
        check_vma=False,
    )
```

```python
import jax
import jax.numpy as jnp
from jax import lax
from jax.experimental import pallas as pl
from jax.experimental.pallas import tpu as pltpu
from jax.sharding import PartitionSpec as P

AXES = ("row", "col")
BF = jnp.bfloat16
F32 = jnp.float32
N = 256


def ring(a, b, n):
    d = (a - b) % n
    return min(d, n - d)


def row_hops(a, b):
    return ring(a // 4, b // 4, 8) + ring(a % 4, b % 4, 4)


def col_hops(a, b):
    return 2 * ring(a // 2, b // 2, 4) + (a % 2 != b % 2)


def spread_pairs(shift):
    pairs = []
    for m in range(4):
        for q in range(8):
            source = 8 * (m ^ shift) + q
            rows = sorted(range(8 * m, 8 * m + 8), key=lambda o: -row_hops(o, source))
            cols = sorted(range(8), key=lambda t: col_hops(t, q))
            pairs += [(source * 8 + t, o * 8 + q) for o, t in zip(rows, cols)]
    return sorted(pairs)


def turn_table():
    table = []
    for r in range(8):
        rows = sorted(range(8), key=lambda o: -row_hops(o, r))
        cols = sorted(range(8), key=lambda t: col_hops(t, r))
        line = [0] * 8
        for o, t in zip(rows, cols):
            line[t] = o
        table.append(line)
    return table


def turn_pairs():
    table = turn_table()
    return [
        ((8 * m + r) * 8 + t, (8 * m + table[r][t]) * 8 + r)
        for m in range(4)
        for r in range(8)
        for t in range(8)
    ]


def send(value, pairs):
    return lax.ppermute(value, AXES, pairs)


def dot(tile, block):
    return lax.dot_general(tile, block, (((1,), (1,)), ((), ())), preferred_element_type=F32)


def at(array, index, axis=0):
    return lax.dynamic_index_in_dim(array, index, axis, keepdims=False)


def params(mib=24):
    return pltpu.CompilerParams(vmem_limit_bytes=mib * 1024 * 1024)


def whole(*_):
    return pl.BlockSpec(memory_space=pltpu.VMEM)


def diagonal0(place, near, far, tiles, ready, passed):
    count = len(ready)

    def kernel(s, near_ref, far_ref, tile_ref, *refs):
        e, out_ref = s[1], refs[count + len(passed)]
        for a in range(4):
            value = jnp.dot(tile_ref[a, e], near_ref[a], preferred_element_type=F32)
            value += jnp.dot(tile_ref[a, 1 - e], far_ref[a], preferred_element_type=F32)
            out_ref[:, a] = value.T.reshape(8, 16, 256).astype(BF)

    anywhere = pl.BlockSpec(memory_space=pl.ANY)
    return pl.pallas_call(
        kernel,
        out_shape=(jax.ShapeDtypeStruct((8, 4, 16, 256), BF),)
        + tuple(jax.ShapeDtypeStruct(value.shape, value.dtype) for value in passed),
        in_specs=[pl.BlockSpec(memory_space=pltpu.SMEM), whole(), whole(), whole()]
        + [anywhere] * (count + len(passed)),
        out_specs=(whole(),) + (anywhere,) * len(passed),
        input_output_aliases={4 + count + i: 1 + i for i in range(len(passed))},
        compiler_params=params(),
        name="diagonal0",
    )(place, near, far, tiles, *ready, *passed)


def lower0(place, keep, slices, one, two, last):
    def kernel(s, k, x_ref, one_ref, two_ref, last_ref, out_ref, acc):
        c, h = pl.program_id(0), s[3]

        def term(pairs):
            tiles = jnp.concatenate([tile for _, tile, _ in pairs], axis=1)
            blocks = []
            for a0, _, flag in pairs:
                block = jnp.concatenate([x_ref[p % 4, p // 4, a0] for p in range(8)], axis=0)
                blocks.append(jnp.where(flag != 0, block, jnp.zeros_like(block)))
            return dot(tiles, jnp.concatenate(blocks, axis=1))

        sums = [
            term([(h, one_ref[0, 0], k[4 * h + c])]),
            term([(2 + h, one_ref[1, 0], k[32 + 8 + 4 * h + c])]),
            term([(2 * h + b, two_ref[b, 0], k[64 + 8 * h + 4 * b + c]) for b in range(2)]),
            term([(a0, last_ref[a0, 0], k[96 + 4 * a0 + c]) for a0 in range(4)]),
        ]

        @pl.when(c == 0)
        def _():
            for i in range(4):
                acc[i] = sums[i]

        @pl.when(c != 0)
        def _():
            for i in range(4):
                acc[i] += sums[i]

        @pl.when(c == 3)
        def _():
            for i in range(4):
                value = acc[i].T.astype(BF)
                for p in range(8):
                    out_ref[s[4 + p], i] = value[16 * p : 16 * p + 16]

    return pl.pallas_call(
        kernel,
        out_shape=jax.ShapeDtypeStruct((8, 4, 16, 256), BF),
        grid_spec=pltpu.PrefetchScalarGridSpec(
            num_scalar_prefetch=2,
            grid=(4,),
            in_specs=[
                pl.BlockSpec((4, 2, 4, 16, 256), lambda c, s, k: (0, c, 0, 0, 0)),
                pl.BlockSpec((2, 1, 256, 256), lambda c, s, k: (0, c, 0, 0)),
                pl.BlockSpec((2, 1, 256, 256), lambda c, s, k: (0, c, 0, 0)),
                pl.BlockSpec((4, 1, 256, 256), lambda c, s, k: (0, c, 0, 0)),
            ],
            out_specs=pl.BlockSpec((8, 4, 16, 256), lambda c, s, k: (0, 0, 0, 0)),
            scratch_shapes=[pltpu.VMEM((4, 256, 128), F32)],
        ),
        compiler_params=params(),
        name="lower0",
    )(place, keep, slices, one, two, last)


def multiply(place, terms, base, n_out, copies, name, dtype=BF, early=None):
    steps = terms[0][3]
    early = early or ()
    lead = sum(value.shape[0] for value in early)
    total = n_out if not early else 8

    def kernel(s, *refs):
        step = pl.program_id(0)
        copy_ref, out_ref, acc = refs[-3:]
        h = s[3]
        tiles, blocks = [[] for _ in range(n_out)], [[] for _ in range(n_out)]
        for n, (_, _, _, _, _, picks) in enumerate(terms):
            x_ref, tile_ref = refs[2 * n : 2 * n + 2]
            for t, c, a, o in picks(step, h):
                for j in range(8):
                    tiles[o].append(tile_ref[j, t])
                    blocks[o].append(x_ref[8 * c + j, a])
        for o in range(n_out):
            value = dot(jnp.concatenate(tiles[o], axis=1), jnp.concatenate(blocks[o], axis=1))

            @pl.when(step == 0)
            def _():
                acc[o] = value

            @pl.when(step != 0)
            def _():
                acc[o] += value

        @pl.when(step == steps - 1)
        def _():
            for o in range(n_out):
                value = acc[o].T
                if base is not None:
                    value = refs[2 * len(terms)][o] - value
                out_ref[lead + o] = value
                cast = value.astype(dtype)
                for r in range(copies):
                    copy_ref[r, o] = cast
            if early:
                out_ref[0:4] = refs[2 * len(terms)][...]
                out_ref[4:6] = refs[2 * len(terms) + 1][...]
                out_ref[7:8] = jnp.zeros((1, 16, 256), F32)

    args, specs, size = [], [], 0
    for x, tiles, first, _, count, _ in terms:
        args += [x, tiles]
        specs.append(pl.BlockSpec(x.shape, lambda i, s: (0, 0, 0, 0)))
        specs.append(
            pl.BlockSpec((8, count, 256, 256), lambda i, s, f=first // count: (0, f + i, 0, 0))
        )
        size += 8 * count * steps * 256 * 256
    if base is not None:
        args.append(base)
        specs.append(pl.BlockSpec(base.shape, lambda i, s: (0, 0, 0)))
    for value in early:
        args.append(value)
        specs.append(pl.BlockSpec(value.shape, lambda i, s: (0, 0, 0)))
    return pl.pallas_call(
        kernel,
        out_shape=(
            jax.ShapeDtypeStruct((copies, n_out, 16, 256), dtype),
            jax.ShapeDtypeStruct((total, 16, 256), F32),
        ),
        grid_spec=pltpu.PrefetchScalarGridSpec(
            num_scalar_prefetch=1,
            grid=(steps,),
            in_specs=specs,
            out_specs=(
                pl.BlockSpec((copies, n_out, 16, 256), lambda i, s: (0, 0, 0, 0)),
                pl.BlockSpec((total, 16, 256), lambda i, s: (0, 0, 0)),
            ),
            scratch_shapes=[pltpu.VMEM((n_out, 256, 16), F32)],
        ),
        compiler_params=params(),
        cost_estimate=pl.CostEstimate(flops=256 * size, bytes_accessed=2 * size, transcendentals=0),
        name=name,
    )(place, *args)


def assemble_early(slices):
    def kernel(x_ref, out_ref):
        out_ref[0] = x_ref[:, 0].reshape(128, 256).T

    return pl.pallas_call(
        kernel,
        out_shape=jax.ShapeDtypeStruct((8, 256, 128), F32),
        grid=(7,),
        in_specs=[pl.BlockSpec((8, 1, 16, 256), lambda i: (0, i, 0, 0))],
        out_specs=pl.BlockSpec((1, 256, 128), lambda i: (i, 0, 0)),
        compiler_params=params(),
        name="assemble_early",
    )(slices)


def assemble_late(early, slices):
    def kernel(x_ref, _, out_ref):
        out_ref[0] = x_ref[:, 0].reshape(128, 256).T

    return pl.pallas_call(
        kernel,
        out_shape=jax.ShapeDtypeStruct((8, 256, 128), F32),
        grid=(1,),
        in_specs=[
            pl.BlockSpec((8, 1, 16, 256), lambda i: (0, i, 0, 0)),
            pl.BlockSpec(memory_space=pl.ANY),
        ],
        out_specs=pl.BlockSpec((1, 256, 128), lambda i: (7 + i, 0, 0)),
        input_output_aliases={1: 0},
        compiler_params=params(),
        name="assemble_late",
    )(slices, early)


HALVES = [list(range(16)), list(range(16, 32))]
ALONG_Z = [[4 * z + x for z in range(8)] for x in range(4)]
ALONG_X = [[4 * z + x for x in range(4)] for z in range(8)]


def exchange(copies, axis, groups=None):
    return lax.all_to_all(copies, axis, 0, 0, tiled=True, axis_index_groups=groups)


def swap(value, mask):
    return send(value, [(i, i ^ mask) for i in range(256)])


def finish0(sums, upper):
    def kernel(x_ref, upper_ref, copy_ref, two_ref, three_ref):
        value = upper_ref[...] - jnp.sum(x_ref[...].astype(F32), axis=0)
        two_ref[...] = value[2:3]
        three_ref[...] = value[3:4]
        cast = value[0:2].astype(BF)
        for r in range(16):
            copy_ref[r] = cast

    slot = jax.ShapeDtypeStruct((1, 16, 256), F32)
    return pl.pallas_call(
        kernel,
        out_shape=(jax.ShapeDtypeStruct((16, 2, 16, 256), BF), slot, slot),
        compiler_params=params(),
        name="finish0",
    )(sums, upper)


def body(rhs, inverse_low, inverse_top, lower_one, lower_two, lower_top, block_rows):
    row = lax.axis_index("row")
    col = lax.axis_index("col")
    m, h, e, core = row // 8, row // 16, row // 8 % 2, col % 2
    table = turn_table()
    owner = [[line.index(p) for p in range(8)] for line in table]
    place = jnp.concatenate(
        [jnp.stack([m, e, core, h]), at(jnp.array(owner, jnp.int32), col), col[None]]
    ).astype(jnp.int32)
    sent0 = rhs[0:4, 0].astype(BF)
    near = send(sent0, spread_pairs(0))
    far = send(sent0, spread_pairs(1))

    lists = at(block_rows.reshape(32, 8, 64), col, 1)

    def listed(block_row, first, count):
        return jnp.any(lax.dynamic_slice(lists, (first, 0), (count, 64)) == block_row, axis=-1)

    def masked(tiles, flags):
        return jnp.where(flags[:, None, None], tiles, jnp.zeros_like(tiles))

    low = jnp.swapaxes(inverse_low[0:4, 0, :, :, 0, :], 1, 2)
    upper_low = jnp.swapaxes(inverse_low[4:7, 0, :, :, 0, :], 1, 2)
    two = jnp.swapaxes(lower_two[0, 0, :, :, 0, :], 0, 1).reshape(3, 4, 256, 256)
    last = jnp.swapaxes(lower_top[0, 0, :, :, 0, :], 0, 1).reshape(7, 4, 256, 256)
    low1, low2 = upper_low[0:2].reshape(4, 256, 256), upper_low[2]
    two1 = masked(two[2], listed(192 + row, 16 + 4 * h, 4))
    first = lax.all_gather(jnp.concatenate([low1, two1, low2]), "col")
    one = jnp.swapaxes(lower_one[:, 0, :, :, 0, :], 1, 2)
    upper = lax.dynamic_slice(jnp.swapaxes(rhs[4:8, 0], 1, 2), (0, 16 * col, 0), (4, 16, 256))
    targets = jnp.stack([128 + row, 160 + row, 192 + row, 224 + row])
    keep = jnp.any(lists[None] == targets[:, None, None], axis=-1).astype(jnp.int32).reshape(128)

    second = masked(last[4:7].reshape(12, 256, 256), listed(224 + row, 16, 12))
    third = jnp.swapaxes(inverse_top[0, 0, :, :, 0, :], 0, 1)

    part, second, third = diagonal0(place, near, far, low, (one, upper, keep), (second, third))
    second, third = [lax.all_gather(value, "col") for value in (second, third)]
    sums = exchange(part, "col")
    solved0 = jnp.sum(sums.astype(F32), axis=0)
    slices = send(solved0.astype(BF), turn_pairs())
    slices = exchange(jnp.broadcast_to(slices, (8, 4, 16, 256)), "row", ALONG_Z)
    slices = exchange(jnp.broadcast_to(slices, (4, 8, 4, 16, 256)), "row", ALONG_X)
    sums = exchange(lower0(place, keep, slices, one, two, last), "col")
    copies, base2, base3 = finish0(sums, upper)

    reduced = exchange(copies, "row", HALVES)
    copies, solved1 = multiply(
        place, [(reduced, first, 0, 1, 4, lambda i, h: [(t, t % 2, t // 2, t // 2) for t in range(4)])], None, 2, 32, "diagonal1"
    )
    x1 = exchange(copies, "row")

    copies, _ = multiply(
        place, [(x1, first, 4, 4, 1, lambda i, h: [(0, i, h, 0)])], base2, 1, 16, "lower2"
    )
    reduced = exchange(copies, "row", HALVES)
    copies, solved2 = multiply(
        place, [(reduced, first, 8, 2, 1, lambda i, h: [(0, i, 0, 0)])], None, 1, 32, "diagonal2", early=(solved0, solved1)
    )
    x2 = exchange(copies, "row")
    early = lax.all_gather(solved2, "col")

    copies, _ = multiply(
        place,
        [
            (x1, second, 0, 4, 2, lambda i, h: [(t, (2 * i + t) % 4, i // 2, 0) for t in range(2)]),
            (x2, second, 8, 4, 1, lambda i, h: [(0, i, 0, 0)]),
        ],
        base3, 1, 32, "lower3",
    )
    reduced = exchange(copies, "row")
    copies, _ = multiply(
        place, [(reduced, third, 0, 4, 1, lambda i, h: [(0, i, 0, 0)])], None, 1, 8, "diagonal3", dtype=F32
    )
    late = exchange(copies, "col")
    return assemble_late(assemble_early(early), late)[:, None]


def solution(mesh):
    return jax.shard_map(
        body,
        mesh=mesh,
        in_specs=(
            P(None, "row", None, None),
            P(None, "row", None, None, "col", None),
            P(None, "row", None, None, "col", None),
            P(None, "row", None, None, "col", None),
            P(None, "row", None, None, "col", None),
            P(None, "row", None, None, "col", None),
            P(),
        ),
        out_specs=P(None, "row", None, None),
        check_vma=False,
    )
```

```python
import jax
import jax.numpy as jnp
from jax import lax
from jax.experimental import pallas as pl
from jax.experimental.pallas import tpu as pltpu
from jax.sharding import PartitionSpec as P

AXES = ("row", "col")
BF = jnp.bfloat16
F32 = jnp.float32
N = 256


def ring(a, b, n):
    d = (a - b) % n
    return min(d, n - d)


def row_hops(a, b):
    return ring(a // 4, b // 4, 8) + ring(a % 4, b % 4, 4)


def col_hops(a, b):
    return 2 * ring(a // 2, b // 2, 4) + (a % 2 != b % 2)


def spread_pairs(shift):
    pairs = []
    for m in range(4):
        for q in range(8):
            source = 8 * (m ^ shift) + q
            rows = sorted(range(8 * m, 8 * m + 8), key=lambda o: -row_hops(o, source))
            cols = sorted(range(8), key=lambda t: col_hops(t, q))
            pairs += [(source * 8 + t, o * 8 + q) for o, t in zip(rows, cols)]
    return sorted(pairs)


def turn_table():
    table = []
    for r in range(8):
        rows = sorted(range(8), key=lambda o: -row_hops(o, r))
        cols = sorted(range(8), key=lambda t: col_hops(t, r))
        line = [0] * 8
        for o, t in zip(rows, cols):
            line[t] = o
        table.append(line)
    return table


def turn_pairs():
    table = turn_table()
    return [
        ((8 * m + r) * 8 + t, (8 * m + table[r][t]) * 8 + r)
        for m in range(4)
        for r in range(8)
        for t in range(8)
    ]


def send(value, pairs):
    return lax.ppermute(value, AXES, pairs)


def dot(tile, block):
    return lax.dot_general(tile, block, (((1,), (1,)), ((), ())), preferred_element_type=F32)


def at(array, index, axis=0):
    return lax.dynamic_index_in_dim(array, index, axis, keepdims=False)


def params(mib=24):
    return pltpu.CompilerParams(vmem_limit_bytes=mib * 1024 * 1024)


def whole(*_):
    return pl.BlockSpec(memory_space=pltpu.VMEM)


def diagonal0(place, near, far, tiles, ready, passed):
    count = len(ready)

    def kernel(s, near_ref, far_ref, tile_ref, *refs):
        e, out_ref = s[1], refs[count + len(passed)]
        for a in range(4):
            value = jnp.dot(tile_ref[a, e], near_ref[a], preferred_element_type=F32)
            value += jnp.dot(tile_ref[a, 1 - e], far_ref[a], preferred_element_type=F32)
            out_ref[:, a] = value.T.reshape(8, 16, 256).astype(BF)

    anywhere = pl.BlockSpec(memory_space=pl.ANY)
    return pl.pallas_call(
        kernel,
        out_shape=(jax.ShapeDtypeStruct((8, 4, 16, 256), BF),)
        + tuple(jax.ShapeDtypeStruct(value.shape, value.dtype) for value in passed),
        in_specs=[pl.BlockSpec(memory_space=pltpu.SMEM), whole(), whole(), whole()]
        + [anywhere] * (count + len(passed)),
        out_specs=(whole(),) + (anywhere,) * len(passed),
        input_output_aliases={4 + count + i: 1 + i for i in range(len(passed))},
        compiler_params=params(),
        name="diagonal0",
    )(place, near, far, tiles, *ready, *passed)


def lower0(place, keep, slices, one, two, last):
    def kernel(s, k, x_ref, one_ref, two_ref, last_ref, out_ref, acc):
        c, h = pl.program_id(0), s[3]

        def term(pairs):
            tiles = jnp.concatenate([tile for _, tile, _ in pairs], axis=1)
            blocks = []
            for a0, _, flag in pairs:
                block = jnp.concatenate([x_ref[p % 4, p // 4, a0] for p in range(8)], axis=0)
                blocks.append(jnp.where(flag != 0, block, jnp.zeros_like(block)))
            return dot(tiles, jnp.concatenate(blocks, axis=1))

        sums = [
            term([(h, one_ref[0, 0], k[4 * h + c])]),
            term([(2 + h, one_ref[1, 0], k[32 + 8 + 4 * h + c])]),
            term([(2 * h + b, two_ref[b, 0], k[64 + 8 * h + 4 * b + c]) for b in range(2)]),
            term([(a0, last_ref[a0, 0], k[96 + 4 * a0 + c]) for a0 in range(4)]),
        ]

        @pl.when(c == 0)
        def _():
            for i in range(4):
                acc[i] = sums[i]

        @pl.when(c != 0)
        def _():
            for i in range(4):
                acc[i] += sums[i]

        @pl.when(c == 3)
        def _():
            for i in range(4):
                value = acc[i].T.astype(BF)
                for p in range(8):
                    out_ref[s[4 + p], i] = value[16 * p : 16 * p + 16]

    return pl.pallas_call(
        kernel,
        out_shape=jax.ShapeDtypeStruct((8, 4, 16, 256), BF),
        grid_spec=pltpu.PrefetchScalarGridSpec(
            num_scalar_prefetch=2,
            grid=(4,),
            in_specs=[
                pl.BlockSpec((4, 2, 4, 16, 256), lambda c, s, k: (0, c, 0, 0, 0)),
                pl.BlockSpec((2, 1, 256, 256), lambda c, s, k: (0, c, 0, 0)),
                pl.BlockSpec((2, 1, 256, 256), lambda c, s, k: (0, c, 0, 0)),
                pl.BlockSpec((4, 1, 256, 256), lambda c, s, k: (0, c, 0, 0)),
            ],
            out_specs=pl.BlockSpec((8, 4, 16, 256), lambda c, s, k: (0, 0, 0, 0)),
            scratch_shapes=[pltpu.VMEM((4, 256, 128), F32)],
        ),
        compiler_params=params(),
        name="lower0",
    )(place, keep, slices, one, two, last)


def multiply(place, terms, base, n_out, copies, name, dtype=BF, early=None, halves=False, extra=None):
    steps = terms[0][3]
    early = early or ()
    lead = sum(value.shape[0] for value in early)
    total = n_out if not early else 8

    def kernel(s, *refs):
        step = pl.program_id(0)
        copy_ref, out_ref, acc = (*refs[-4:-2], refs[-1]) if halves else refs[-3:]
        h = s[3]
        tiles, blocks = [[] for _ in range(n_out)], [[] for _ in range(n_out)]
        for n, (_, _, _, _, _, picks) in enumerate(terms):
            x_ref, tile_ref = refs[2 * n : 2 * n + 2]
            for t, c, a, o, *other in picks(step, h):
                for j in range(8):
                    tiles[o].append(tile_ref[j, t])
                    block = x_ref[8 * c + j, a]
                    if other:
                        block = jnp.where(h == other[0], block, refs[2 * other[1]][8 * c + j, 1])
                    blocks[o].append(block)
        for o in range(n_out):
            value = dot(jnp.concatenate(tiles[o], axis=1), jnp.concatenate(blocks[o], axis=1))

            @pl.when(step == 0)
            def _():
                acc[o] = value

            @pl.when(step != 0)
            def _():
                acc[o] += value

        @pl.when(step == steps - 1)
        def _():
            for o in range(n_out):
                value = acc[o].T
                if base is not None:
                    value = refs[2 * len(terms)][o] - value
                out_ref[lead + o] = value
                cast = value.astype(dtype)
                for r in range(copies):
                    if not halves:
                        copy_ref[r, o] = cast
                    elif r // 16 == o:
                        copy_ref[r, 0] = cast
                    else:
                        refs[-2][r, 0] = cast
            if extra is not None:
                copy_ref[:, n_out : n_out + 1] = refs[-4][...]
            if early:
                out_ref[0:4] = refs[2 * len(terms)][...]
                out_ref[4:6] = refs[2 * len(terms) + 1][...]
                out_ref[7:8] = jnp.zeros((1, 16, 256), F32)

    args, specs, size = [], [], 0
    for x, tiles, first, _, count, _ in terms:
        args += [x, tiles]
        specs.append(pl.BlockSpec(x.shape, lambda i, s: (0, 0, 0, 0)))
        specs.append(
            pl.BlockSpec((8, count, 256, 256), lambda i, s, f=first // count: (0, f + i, 0, 0))
        )
        size += 8 * count * steps * 256 * 256
    if base is not None:
        args.append(base)
        specs.append(pl.BlockSpec(base.shape, lambda i, s: (0, 0, 0)))
    for value in early:
        args.append(value)
        specs.append(pl.BlockSpec(value.shape, lambda i, s: (0, 0, 0)))
    if extra is not None:
        args.append(extra)
        specs.append(pl.BlockSpec(extra.shape, lambda i, s: (0, 0, 0, 0)))
    wide = 1 if halves else n_out + (extra is not None)
    apart = ((copies, 1, 16, 256),) if halves else ()
    return pl.pallas_call(
        kernel,
        out_shape=(
            jax.ShapeDtypeStruct((copies, wide, 16, 256), dtype),
            jax.ShapeDtypeStruct((total, 16, 256), F32),
        )
        + tuple(jax.ShapeDtypeStruct(shape, BF) for shape in apart),
        grid_spec=pltpu.PrefetchScalarGridSpec(
            num_scalar_prefetch=1,
            grid=(steps,),
            in_specs=specs,
            out_specs=(
                pl.BlockSpec((copies, wide, 16, 256), lambda i, s: (0, 0, 0, 0)),
                pl.BlockSpec((total, 16, 256), lambda i, s: (0, 0, 0)),
            )
            + tuple(pl.BlockSpec(shape, lambda i, s: (0, 0, 0, 0)) for shape in apart),
            scratch_shapes=[pltpu.VMEM((n_out, 256, 16), F32)],
        ),
        compiler_params=params(),
        cost_estimate=pl.CostEstimate(flops=256 * size, bytes_accessed=2 * size, transcendentals=0),
        name=name,
    )(place, *args)


def assemble_early(tiles):
    def kernel(high_ref, fine_ref, out_ref):
        value = high_ref[:, 0].astype(F32) + fine_ref[:, 0].astype(F32)
        out_ref[0] = value.reshape(128, 256).T

    return pl.pallas_call(
        kernel,
        out_shape=jax.ShapeDtypeStruct((8, 256, 128), F32),
        grid=(7,),
        in_specs=[
            pl.BlockSpec((8, 1, 16, 256), lambda i: (0, 4, i, 0)),
            pl.BlockSpec((8, 1, 16, 256), lambda i: (0, 4, 8 + i, 0)),
        ],
        out_specs=pl.BlockSpec((1, 256, 128), lambda i: (i, 0, 0)),
        compiler_params=params(56),
        name="assemble_early",
    )(tiles, tiles)


def assemble_late(early, slices):
    def kernel(x_ref, _, out_ref):
        out_ref[0] = x_ref[:, 0].reshape(128, 256).T

    return pl.pallas_call(
        kernel,
        out_shape=jax.ShapeDtypeStruct((8, 256, 128), F32),
        grid=(1,),
        in_specs=[
            pl.BlockSpec((8, 1, 16, 256), lambda i: (0, i, 0, 0)),
            pl.BlockSpec(memory_space=pl.ANY),
        ],
        out_specs=pl.BlockSpec((1, 256, 128), lambda i: (7 + i, 0, 0)),
        input_output_aliases={1: 0},
        compiler_params=params(),
        name="assemble_late",
    )(slices, early)


HALVES = [list(range(16)), list(range(16, 32))]
ALONG_Z = [[4 * z + x for z in range(8)] for x in range(4)]
ALONG_X = [[4 * z + x for x in range(4)] for z in range(8)]


def exchange(copies, axis, groups=None):
    return lax.all_to_all(copies, axis, 0, 0, tiled=True, axis_index_groups=groups)


def swap(value, mask):
    return send(value, [(i, i ^ mask) for i in range(256)])


def finish0(sums, upper):
    def kernel(x_ref, upper_ref, copy_ref, two_ref, three_ref):
        value = upper_ref[...] - jnp.sum(x_ref[...].astype(F32), axis=0)
        two_ref[...] = value[2:3]
        three_ref[...] = value[3:4]
        cast = value[0:2].astype(BF)
        for r in range(16):
            copy_ref[r] = cast

    slot = jax.ShapeDtypeStruct((1, 16, 256), F32)
    return pl.pallas_call(
        kernel,
        out_shape=(jax.ShapeDtypeStruct((16, 2, 16, 256), BF), slot, slot),
        compiler_params=params(),
        name="finish0",
    )(sums, upper)


def body(rhs, inverse_low, inverse_top, lower_one, lower_two, lower_top, block_rows):
    row = lax.axis_index("row")
    col = lax.axis_index("col")
    m, h, e, core = row // 8, row // 16, row // 8 % 2, col % 2
    table = turn_table()
    owner = [[line.index(p) for p in range(8)] for line in table]
    place = jnp.concatenate(
        [jnp.stack([m, e, core, h]), at(jnp.array(owner, jnp.int32), col), col[None]]
    ).astype(jnp.int32)
    sent0 = rhs[0:4, 0].astype(BF)
    near = send(sent0, spread_pairs(0))
    far = send(sent0, spread_pairs(1))

    lists = at(block_rows.reshape(32, 8, 64), col, 1)

    def listed(block_row, first, count):
        return jnp.any(lax.dynamic_slice(lists, (first, 0), (count, 64)) == block_row, axis=-1)

    def masked(tiles, flags):
        return jnp.where(flags[:, None, None], tiles, jnp.zeros_like(tiles))

    low = jnp.swapaxes(inverse_low[0:4, 0, :, :, 0, :], 1, 2)
    upper_low = jnp.swapaxes(inverse_low[4:7, 0, :, :, 0, :], 1, 2)
    two = jnp.swapaxes(lower_two[0, 0, :, :, 0, :], 0, 1).reshape(3, 4, 256, 256)
    last = jnp.swapaxes(lower_top[0, 0, :, :, 0, :], 0, 1).reshape(7, 4, 256, 256)
    low1, low2 = upper_low[0:2].reshape(4, 256, 256), upper_low[2]
    two1 = masked(two[2], listed(192 + row, 16 + 4 * h, 4))
    first = lax.all_gather(jnp.concatenate([low1, two1, low2]), "col")
    one = jnp.swapaxes(lower_one[:, 0, :, :, 0, :], 1, 2)
    upper = lax.dynamic_slice(jnp.swapaxes(rhs[4:8, 0], 1, 2), (0, 16 * col, 0), (4, 16, 256))
    targets = jnp.stack([128 + row, 160 + row, 192 + row, 224 + row])
    keep = jnp.any(lists[None] == targets[:, None, None], axis=-1).astype(jnp.int32).reshape(128)

    second = masked(last[4:7].reshape(12, 256, 256), listed(224 + row, 16, 12))
    third = jnp.pad(jnp.swapaxes(inverse_top[0, 0, :, :, 0, :], 0, 1), ((0, 1), (0, 0), (0, 0)))

    part, second, third = diagonal0(place, near, far, low, (one, upper, keep), (second, third))
    second = lax.all_gather(second, "col")
    sums = exchange(part, "col")
    solved0 = jnp.sum(sums.astype(F32), axis=0)
    slices = send(solved0.astype(BF), turn_pairs())
    slices = exchange(jnp.broadcast_to(slices, (8, 4, 16, 256)), "row", ALONG_Z)
    slices = exchange(jnp.broadcast_to(slices, (4, 8, 4, 16, 256)), "row", ALONG_X)
    sums = exchange(lower0(place, keep, slices, one, two, last), "col")
    copies, base2, base3 = finish0(sums, upper)

    reduced = exchange(copies, "row", HALVES)
    copies, solved1, other1 = multiply(
        place, [(reduced, first, 0, 1, 4, lambda i, h: [(t, t % 2, t // 2, t // 2) for t in range(4)])], None, 2, 32, "diagonal1", halves=True
    )
    x1 = exchange(copies, "row")

    copies, _ = multiply(
        place, [(x1, first, 4, 4, 1, lambda i, h: [(0, i, 0, 0)])], base2, 1, 16, "lower2"
    )
    reduced = exchange(copies, "row", HALVES)
    copies, solved2 = multiply(
        place, [(reduced, first, 8, 2, 1, lambda i, h: [(0, i, 0, 0)])], None, 1, 32, "diagonal2", early=(solved0, solved1), extra=other1
    )
    x2 = exchange(copies, "row")
    high = solved2.astype(BF)
    fine = (solved2 - high.astype(F32)).astype(BF)
    early = jnp.concatenate([high, fine]).reshape(1, 256, 256)
    third = lax.all_gather(lax.dynamic_update_slice(third, early, (4, 0, 0)), "col")

    copies, _ = multiply(
        place,
        [
            (x1, second, 0, 4, 2, lambda i, h: [(t, (2 * i + t) % 4, 0, 0, i // 2, 1) for t in range(2)]),
            (x2, second, 8, 4, 1, lambda i, h: [(0, i, 0, 0)]),
        ],
        base3, 1, 32, "lower3",
    )
    reduced = exchange(copies, "row")
    copies, _ = multiply(
        place, [(reduced, third, 0, 4, 1, lambda i, h: [(0, i, 0, 0)])], None, 1, 8, "diagonal3", dtype=F32
    )
    late = exchange(copies, "col")
    return assemble_late(assemble_early(third), late)[:, None]


def solution(mesh):
    return jax.shard_map(
        body,
        mesh=mesh,
        in_specs=(
            P(None, "row", None, None),
            P(None, "row", None, None, "col", None),
            P(None, "row", None, None, "col", None),
            P(None, "row", None, None, "col", None),
            P(None, "row", None, None, "col", None),
            P(None, "row", None, None, "col", None),
            P(),
        ),
        out_specs=P(None, "row", None, None),
        check_vma=False,
    )
```
